32 devices in a mesh: row: 4 (over x, core), col: 8 (over z, y).
Axes of the slice: x: 2, y: 2, z: 4, core: 2. Of those that a mesh axis runs over, the one named last changes fastest.
Arguments:
- basis: bfloat16 [2, 8, 1536, 384], P(None, 'col', 'row'), may hold values from -0.078125 to 0.078125
- offsets: bfloat16 [2, 8, 3, 1536], P(None, 'col', None, 'row'), may hold values from -1 to 1
- centers: float32 [16, 3], replicated, may hold values from -1 to 16
- patch_points: int32 [16], replicated, may hold values from 768 to 1536, as said below
- base: float32 [4, 4, 128, 2, 8, 128], P(None, 'row', None, None, 'col'), may hold values from -1 to 33
Outputs:
- factored: float32 [4, 4, 128, 2, 8, 128], P(None, 'row', None, None, 'col')
The draws below stay inside these ranges and needn't reach their ends.
Inputs may be any that keep to these rules, and one draw needn't show every extreme that they name: `patch_points`: every patch has at least 768 live points, and some patch has exactly 1536.
All inputs are finite; a program needn't handle non-finite values.
Results may differ from the reference program's by a relative error of at most 0.00066.
Values may be sent and summed in bfloat16 or wider, within the bound.
A program may use at most 64 MiB of HBM per device.

```python
import jax
import jax.numpy as jnp
from jax import lax

NB = 128
NCOMP = 3
NMAX = 1536
NMIN = 768
NPATCH = 16
PANEL = 128
NPANEL = 2
WIN = 2048
N_ROW = 4
N_COL = 8


def draw_patch_points(key, part):
    counts = jax.random.randint(jax.random.fold_in(key, 11), (NPATCH,), NMIN, NMAX + 1)
    order = jax.random.permutation(jax.random.fold_in(key, 12), NPATCH)
    counts = counts.at[order[0]].set(NMAX)
    counts = counts.at[order[1]].set(NMIN)
    return counts.astype(jnp.int32)


def draw_centers(key, part):
    index = jnp.arange(NPATCH)
    grid_x = (index % 8).astype(jnp.float32) * 2.0
    grid_y = (index // 8).astype(jnp.float32) * 2.0
    jitter = jnp.clip(0.15 * jax.random.normal(jax.random.fold_in(key, 22), (NPATCH, 3), jnp.float32), -0.6, 0.6)
    grid = jnp.stack([grid_x, grid_y, jnp.zeros_like(grid_x)], axis=1)
    return (grid + jitter + 0.6).astype(jnp.float32)


def draw_offsets(key, part):
    shape = (NPATCH // N_COL, N_COL, 3, NMAX)
    raw = jax.random.uniform(jax.random.fold_in(key, 32), shape, jnp.float32, -1.0, 1.0)
    scale = jnp.array([1.0, 1.0, 0.1], jnp.float32)[None, None, :, None]
    return (raw * scale).astype(jnp.bfloat16)


def draw_base(key, part):
    order = NPATCH * NB
    entries = jnp.clip(jax.random.normal(jax.random.fold_in(key, 42), (order, order), jnp.float32), -6.0, 6.0)
    gains = jnp.exp(jax.random.uniform(jax.random.fold_in(key, 43), (order,), jnp.float32, 0.0, 0.6931))
    rows = jnp.arange(order)[:, None]
    cols = jnp.arange(order)[None, :]
    diagonal = jnp.where(rows == cols, 16.0 * gains[:, None], 0.0)
    matrix = 0.05 * entries + 0.5 + diagonal
    return matrix.reshape(NPATCH // N_ROW, N_ROW, NB, NPATCH // N_COL, N_COL, NB).astype(jnp.float32)


def level_of(stream_key, extent, pieces, smallest, top_value):
    def one(axis_at, parts):
        draws = jax.random.uniform(jax.random.fold_in(jax.random.fold_in(stream_key, 6), axis_at), (parts,), jnp.float32, smallest / len(pieces), top_value / len(pieces))
        return jnp.repeat(jnp.exp(draws), extent[axis_at] // parts).reshape((-1,) + (1,) * (len(extent) - axis_at - 1))

    loudness = one(*pieces[0])
    for cut in pieces[1:]:
        loudness = loudness * one(*cut)
    return loudness


def normal_values(rng, extent, scale, bound, shards=(), kind=jnp.bfloat16):
    values = jax.random.normal(rng, extent, jnp.float32) * scale
    if len(shards) > 0:
        values = level_of(rng, extent, shards, -0.22, 0.18) * values
    return jnp.clip(values, min=-bound, max=bound).astype(kind)


def setup_inputs(seed: int = 0) -> dict:
    streams_of = jax.random.split(jax.random.key(seed), 6)
    return {
        "basis": normal_values(streams_of[0], (NPATCH // N_COL, N_COL, NMAX, NCOMP * NB), (4 * NMAX) ** -0.5, 0.078125, ((1, 8), (2, 4))),
        "offsets": draw_offsets(jax.random.fold_in(streams_of[5], 71), 0),
        "centers": draw_centers(jax.random.fold_in(streams_of[5], 71), 0),
        "patch_points": draw_patch_points(jax.random.fold_in(streams_of[5], 71), 0),
        "base": draw_base(jax.random.fold_in(streams_of[5], 71), 0),
    }


wave_number = 12.0
core_radius = 0.05
highest = lax.Precision.HIGHEST

def kernel_block(row_points, col_points, row_live, col_live):
    squared = jnp.zeros((row_points.shape[1], col_points.shape[1]), jnp.float32)
    for axis_index in range(3):
        spacing = row_points[axis_index][:, None] - col_points[axis_index][None, :]
        squared = squared + spacing * spacing
    value = jnp.cos(wave_number * jnp.sqrt(squared)) / jnp.sqrt(squared + core_radius * core_radius)
    keep = jnp.logical_and(row_live[:, None], col_live[None, :])
    return jnp.where(keep, value, 0.0).astype(jnp.bfloat16)

def unit_lower_inverse(factors):
    order = factors.shape[0]
    if order > 128:
        half = order // 2
        first = unit_lower_inverse(factors[:half, :half])
        second = unit_lower_inverse(factors[half:, half:])
        corner = -jnp.dot(second, jnp.dot(factors[half:, :half], first, precision=highest), precision=highest)
        top = jnp.concatenate([first, jnp.zeros((half, order - half), jnp.float32)], axis=1)
        return jnp.concatenate([top, jnp.concatenate([corner, second], axis=1)], axis=0)
    positions = jnp.arange(order)

    def one_column(column_index, current):
        below = positions > column_index
        multiplier = jnp.where(below, factors[:, column_index], 0.0)
        return current - multiplier[:, None] * current[column_index, :][None, :]
    return lax.fori_loop(0, order, one_column, jnp.eye(order, dtype=jnp.float32))

def upper_inverse(factors):
    order = factors.shape[0]
    if order > 128:
        half = order // 2
        first = upper_inverse(factors[:half, :half])
        second = upper_inverse(factors[half:, half:])
        corner = -jnp.dot(first, jnp.dot(factors[:half, half:], second, precision=highest), precision=highest)
        top = jnp.concatenate([first, corner], axis=1)
        return jnp.concatenate([top, jnp.concatenate([jnp.zeros((order - half, half), jnp.float32), second], axis=1)], axis=0)
    positions = jnp.arange(order)

    def one_column(step, current):
        column_index = order - 1 - step
        scaled_row = current[column_index, :] / factors[column_index, column_index]
        current = current.at[column_index, :].set(scaled_row)
        above = positions < column_index
        multiplier = jnp.where(above, factors[:, column_index], 0.0)
        return current - multiplier[:, None] * scaled_row[None, :]
    return lax.fori_loop(0, order, one_column, jnp.eye(order, dtype=jnp.float32))

def factor_square(matrix):
    order = matrix.shape[0]
    if order > 128:
        half = order // 2
        upper_left = factor_square(matrix[:half, :half])
        lower_left = jnp.dot(matrix[half:, :half], upper_inverse(upper_left), precision=highest)
        upper_right = jnp.dot(unit_lower_inverse(upper_left), matrix[:half, half:], precision=highest)
        rest = factor_square(matrix[half:, half:] - jnp.dot(lower_left, upper_right, precision=highest))
        return jnp.concatenate([jnp.concatenate([upper_left, upper_right], axis=1), jnp.concatenate([lower_left, rest], axis=1)], axis=0)
    positions = jnp.arange(order)

    def one_column(column_index, current):
        pivot = current[column_index, column_index]
        below = positions > column_index
        lower_part = jnp.where(below, current[:, column_index] / pivot, 0.0)
        right_part = jnp.where(below, current[column_index, :], 0.0)
        current = current - lower_part[:, None] * right_part[None, :]
        return current.at[:, column_index].set(jnp.where(below, lower_part, current[:, column_index]))
    return lax.fori_loop(0, order, one_column, matrix)

def reference(basis, offsets, centers, patch_points, base):
    width = NCOMP * NB
    bases = basis.reshape(NPATCH, NMAX, width)
    points = centers[:, :, None] + offsets.reshape(NPATCH, 3, NMAX).astype(jnp.float32)
    live = jnp.arange(NMAX)[None, :] < patch_points[:, None]
    row_points = jnp.transpose(points, (1, 0, 2)).reshape(3, NPATCH * NMAX)
    row_live = live.reshape(-1)
    tests = bases.reshape(NPATCH, NMAX, NCOMP, NB).astype(jnp.float32)

    def column_blocks(patch_q):
        tile = kernel_block(row_points, points[patch_q], row_live, live[patch_q])
        image = jnp.dot(tile, bases[patch_q], preferred_element_type=jnp.float32).astype(jnp.bfloat16)
        image = image.reshape(NPATCH, NMAX, NCOMP, NB).astype(jnp.float32)
        return jnp.einsum('pkcu,pkcv->puv', tests, image)
    blocks = lax.map(column_blocks, jnp.arange(NPATCH))
    reduced = jnp.transpose(blocks, (1, 2, 0, 3)).reshape(WIN, WIN)
    window = base.reshape(WIN, WIN) + reduced
    for panel_index in range(NPANEL):
        start = panel_index * PANEL
        finish = start + PANEL
        diagonal = factor_square(window[start:finish, start:finish])
        left = jnp.dot(window[finish:, start:finish], upper_inverse(diagonal), precision=highest)
        right = jnp.dot(unit_lower_inverse(diagonal), window[start:finish, finish:], precision=highest)
        trailing = window[finish:, finish:] - jnp.dot(left, right, precision=highest)
        window = window.at[start:finish, start:finish].set(diagonal)
        window = window.at[finish:, start:finish].set(left)
        window = window.at[start:finish, finish:].set(right)
        window = window.at[finish:, finish:].set(trailing)
    return window.reshape(base.shape)
```

```python
import jax
import jax.numpy as jnp
import numpy as np
from jax import lax
from jax.experimental import pallas as pl
from jax.experimental.pallas import tpu as pltpu
from jax.sharding import PartitionSpec as P

NB = 128
NCOMP = 3
NMAX = 1536
NPATCH = 16
PANEL = 128
NPANEL = 2


wave_number = 12.0
core_radius = 0.05
highest = lax.Precision.HIGHEST


def kernel_block(row_points, col_points, row_live, col_live):
    squared = jnp.zeros((row_points.shape[1], col_points.shape[1]), jnp.float32)
    for axis_index in range(3):
        spacing = row_points[axis_index][:, None] - col_points[axis_index][None, :]
        squared = squared + spacing * spacing
    value = jnp.cos(wave_number * jnp.sqrt(squared)) / jnp.sqrt(squared + core_radius * core_radius)
    keep = jnp.logical_and(row_live[:, None], col_live[None, :])
    return jnp.where(keep, value, 0.0).astype(jnp.bfloat16)


def panel_kernel(block_ref, factor_ref, lower_ref, upper_ref):
    order = block_ref.shape[0]
    rows = lax.broadcasted_iota(jnp.int32, (order, order), 0)
    cols = lax.broadcasted_iota(jnp.int32, (order, order), 1)
    row_ids = lax.broadcasted_iota(jnp.int32, (order, 1), 0)
    lanes = lax.broadcasted_iota(jnp.int32, (1, order), 1)
    identity = jnp.where(rows == cols, 1.0, 0.0).astype(jnp.float32)
    factor_ref[...] = block_ref[...]
    lower_ref[...] = identity
    upper_ref[...] = identity

    def one_column(k, carry):
        current = factor_ref[...]
        row = factor_ref[pl.ds(k, 1), :]
        lower_row = lower_ref[pl.ds(k, 1), :]
        upper = upper_ref[...]
        at_column = cols == k
        pivot = jnp.sum(jnp.where(lanes == k, row, 0.0), axis=1, keepdims=True)
        column = jnp.sum(jnp.where(at_column, current, 0.0), axis=1, keepdims=True)
        upper_column = jnp.sum(jnp.where(at_column, upper, 0.0), axis=1, keepdims=True)
        multiplier = jnp.where(row_ids > k, column / pivot, 0.0)
        right = jnp.where(lanes > k, row, 0.0)
        factor_ref[...] = jnp.where(
            jnp.logical_and(at_column, rows > k), multiplier, current - multiplier * right
        )
        lower_ref[...] = lower_ref[...] - multiplier * lower_row
        upper_ref[...] = jnp.where(
            at_column, upper_column / pivot, upper - upper_column * (right / pivot)
        )
        return carry

    lax.fori_loop(0, order, one_column, 0)


def factor_panel(block):
    shape = jax.ShapeDtypeStruct(block.shape, jnp.float32)
    spec = pl.BlockSpec(memory_space=pltpu.VMEM)
    return pl.pallas_call(
        panel_kernel,
        out_shape=[shape] * 3,
        in_specs=[spec],
        out_specs=[spec] * 3,
        compiler_params=pltpu.CompilerParams(vmem_limit_bytes=16 * 1024 * 1024),
    )(block)


def local(basis, offsets, centers, patch_points, base):
    row_count = lax.axis_size("row")
    col_count = lax.axis_size("col")
    row_index = lax.axis_index("row")
    col_index = lax.axis_index("col")
    col_blocks = basis.shape[0]
    slice_len = basis.shape[2]
    width = basis.shape[3]
    row_blocks = NPATCH // row_count
    whole_cols, whole_offsets = (
        lax.all_gather(basis, "row", axis=2, tiled=True),
        lax.all_gather(offsets, "row", axis=3, tiled=True),
    )
    source_centers = lax.dynamic_index_in_dim(
        centers.reshape(col_blocks, col_count, 3), col_index, 1, keepdims=False
    )
    source_counts = lax.dynamic_index_in_dim(
        patch_points.reshape(col_blocks, col_count), col_index, 1, keepdims=False
    )
    source_points = source_centers[:, :, None] + whole_offsets[:, 0].astype(jnp.float32)
    source_live = jnp.arange(NMAX)[None, :] < source_counts[:, None]
    source_basis = whole_cols[:, 0]
    sliced, sliced_offsets = (
        lax.all_gather(basis, "col", axis=1, tiled=True),
        lax.all_gather(offsets, "col", axis=1, tiled=True),
    )
    all_slices = sliced.reshape(NPATCH, slice_len, width)
    all_offsets = sliced_offsets.reshape(NPATCH, 3, slice_len)
    class_sizes = patch_points.reshape(row_blocks, row_count)
    class_order = jnp.argsort(-class_sizes, axis=0, stable=True)
    members = jnp.stack(
        [
            jnp.stack(
                [
                    class_order[member, (group - member) % row_count] * row_count
                    + (group - member) % row_count
                    for member in range(row_blocks)
                ]
            )
            for group in range(row_count)
        ]
    )
    flat_members = members.reshape(-1)
    turned_offsets = jnp.transpose(all_offsets, (0, 2, 1))

    def picked(array, ids):
        return jnp.stack(
            [lax.dynamic_index_in_dim(array, ids[n], 0, keepdims=False) for n in range(ids.shape[0])]
        )

    send_basis = picked(all_slices, flat_members)
    send_offsets = picked(turned_offsets, flat_members)
    got_basis, got_offsets = (
        lax.all_to_all(send_basis, "row", split_axis=0, concat_axis=1, tiled=True),
        lax.all_to_all(send_offsets, "row", split_axis=0, concat_axis=1, tiled=True),
    )
    mine = lax.dynamic_index_in_dim(members, row_index, 0, keepdims=False)
    tile_len = 512
    gathered_rows = []
    for member in range(row_blocks):
        patch_id = mine[member]
        live_count = lax.dynamic_index_in_dim(patch_points, patch_id, 0, keepdims=False)
        member_points = lax.dynamic_index_in_dim(centers, patch_id, 0, keepdims=False)[:, None] + got_offsets[member].T.astype(jnp.float32)
        member_live = jnp.arange(NMAX) < live_count
        tile_total = (live_count + tile_len - 1) // tile_len

        def accumulate(
            tile_index, running, member_points=member_points, member_live=member_live, member=member
        ):
            begin = tile_index * tile_len
            row_points = lax.dynamic_slice_in_dim(member_points, begin, tile_len, 1)
            row_live = lax.dynamic_slice_in_dim(member_live, begin, tile_len, 0)
            test_rows = lax.dynamic_slice_in_dim(got_basis[member], begin, tile_len, 0).reshape(
                tile_len, NCOMP, NB
            )
            pieces = []
            for source in range(col_blocks):
                tile = kernel_block(
                    row_points, source_points[source], row_live, source_live[source]
                )
                image = jnp.dot(
                    tile, source_basis[source], preferred_element_type=jnp.float32
                ).astype(jnp.bfloat16)
                image = image.reshape(tile_len, NCOMP, NB)
                pieces.append(
                    jnp.einsum("kcu,kcv->uv", test_rows, image, preferred_element_type=jnp.float32)
                )
            return running + jnp.stack(pieces, axis=1)

        gathered_rows.append(
            lax.fori_loop(0, tile_total, accumulate, jnp.zeros((NB, col_blocks, NB), jnp.float32))
        )
    stacked = jnp.stack(gathered_rows)
    slot_count = (row_blocks + row_count - 1) // row_count
    slot_ids = (np.arange(slot_count) * row_count)[None, :].astype(np.int32)
    peer_ids = jnp.arange(row_count, dtype=jnp.int32)[:, None]
    send_member = slot_ids + (row_index - peer_ids) % row_count
    send_valid = send_member < row_blocks
    outgoing = jnp.where(
        send_valid[:, :, None, None, None], picked(stacked, jnp.minimum(send_member, row_blocks - 1).reshape(-1)).reshape(
            send_member.shape + stacked.shape[1:]
        ), 0.0
    )
    incoming = lax.all_to_all(outgoing, "row", split_axis=0, concat_axis=0, tiled=True)
    recv_member = slot_ids + (peer_ids - row_index) % row_count
    recv_valid = recv_member < row_blocks
    my_order = lax.dynamic_index_in_dim(class_order, row_index, 1, keepdims=False)
    recv_block = jnp.sum(
        jnp.where(
            jnp.minimum(recv_member, row_blocks - 1)[:, :, None] == jnp.arange(row_blocks),
            my_order,
            0,
        ),
        axis=2,
    )
    landing = jnp.logical_and(
        recv_valid[None], recv_block[None] == jnp.arange(row_blocks)[:, None, None]
    ).astype(jnp.float32)
    reduced = jnp.einsum("agt,gtuqv->auqv", landing, incoming, precision=highest).reshape(
        row_blocks, 1, NB, col_blocks, NB
    )
    matrix = (base + reduced.reshape(row_blocks, 1, NB, col_blocks, 1, NB)).reshape(
        row_blocks * NB, col_blocks * NB
    )
    row_global = (
        (jnp.arange(row_blocks)[:, None] * row_count + row_index) * NB + jnp.arange(NB)[None, :]
    ).reshape(-1)
    col_global = (
        (jnp.arange(col_blocks)[:, None] * col_count + col_index) * NB + jnp.arange(NB)[None, :]
    ).reshape(-1)
    for panel_index in range(NPANEL):
        start = panel_index * PANEL
        finish = start + PANEL
        panel_span = start + jnp.arange(PANEL)
        pick_cols = (col_global[:, None] == panel_span[None, :]).astype(jnp.float32)
        pick_rows = (panel_span[:, None] == row_global[None, :]).astype(jnp.float32)
        col_part = jnp.dot(matrix, pick_cols, precision=highest)
        col_panel = lax.psum(col_part, "col")
        diagonal_part = jnp.dot(pick_rows, col_panel, precision=highest)
        row_part = jnp.dot(pick_rows, matrix, precision=highest)
        diagonal_block, row_panel = lax.psum((diagonal_part, row_part), "row")
        factored_block, lower_inverse, upper_inverse = factor_panel(diagonal_block)
        left = jnp.dot(col_panel, upper_inverse, precision=highest)
        right = jnp.dot(lower_inverse, row_panel, precision=highest)
        left_kept = jnp.where((row_global >= finish)[:, None], left, 0.0)
        right_kept = jnp.where((col_global >= finish)[None, :], right, 0.0)
        matrix = matrix - jnp.dot(left_kept, right_kept, precision=highest)
        diagonal_rows = jnp.dot(pick_rows.T, factored_block, precision=highest)
        new_columns = jnp.where(
            (row_global < start)[:, None],
            col_panel,
            jnp.where((row_global < finish)[:, None], diagonal_rows, left),
        )
        in_columns = jnp.logical_and(col_global >= start, col_global < finish)
        matrix = jnp.where(
            in_columns[None, :], jnp.dot(new_columns, pick_cols.T, precision=highest), matrix
        )
        in_rows = jnp.logical_and(row_global >= start, row_global < finish)
        upper_rows = jnp.dot(pick_rows.T, right, precision=highest)
        matrix = jnp.where(
            jnp.logical_and(in_rows[:, None], (col_global >= finish)[None, :]), upper_rows, matrix
        )
    return matrix.reshape(row_blocks, 1, NB, col_blocks, 1, NB)


def solution(mesh):
    in_specs = (
        P(None, "col", "row", None),
        P(None, "col", None, "row"),
        P(),
        P(),
        P(None, "row", None, None, "col", None),
    )
    out_specs = P(None, "row", None, None, "col", None)
    return jax.shard_map(local, mesh=mesh, in_specs=in_specs, out_specs=out_specs, check_vma=False)
```

```python
import math

import jax
import jax.numpy as jnp
import numpy as np
from jax import lax
from jax.experimental import pallas as pl
from jax.experimental.pallas import tpu as pltpu
from jax.sharding import PartitionSpec as P

NB = 128
NCOMP = 3
NMAX = 1536
NPATCH = 16
PANEL = 128
NPANEL = 2


wave_number = 12.0
core_radius = 0.05
highest = lax.Precision.HIGHEST


cosine_series = (0.9999999890590201, -19.739204499453688, 64.93911745988827, -85.45013953077586, 60.16763095018129, -25.96759924584206, 6.528658157862129)
row_tile = 256
col_tile = 256


def pair_kernel(
    row_counts, col_counts, row_points_ref, col_points_ref, test_ref, basis_ref, out_ref, image_ref
):
    member, source, tile = pl.program_id(0), pl.program_id(1), pl.program_id(2)

    @pl.when(tile == 0)
    def _():
        out_ref[...] = jnp.zeros_like(out_ref)

    @pl.when(tile * row_tile < row_counts[member])
    def _():
        image_ref[...] = jnp.zeros_like(image_ref)
        row_points = row_points_ref[0]

        def one_chunk(chunk, carry):
            span = pl.ds(pl.multiple_of(chunk * col_tile, col_tile), col_tile)
            squared = jnp.zeros((row_tile, col_tile), jnp.float32)
            for axis in range(3):
                spacing = row_points[:, axis : axis + 1] - col_points_ref[0, axis : axis + 1, span]
                squared = squared + spacing * spacing
            distance = squared * lax.rsqrt(jnp.maximum(squared, 1e-30))
            turns = distance * (wave_number / (2.0 * math.pi))
            turns = turns - jnp.round(turns)
            square = turns * turns
            cosine = jnp.full_like(square, cosine_series[-1])
            for coefficient in cosine_series[-2::-1]:
                cosine = cosine * square + coefficient
            value = cosine * lax.rsqrt(squared + core_radius * core_radius)
            image_ref[...] += jnp.dot(
                value.astype(jnp.bfloat16), basis_ref[0, span, :], preferred_element_type=jnp.float32
            )
            return carry

        lax.fori_loop(0, (col_counts[source] + col_tile - 1) // col_tile, one_chunk, 0)
        image = image_ref[...].astype(jnp.bfloat16)
        total = out_ref[0, 0]
        for part in range(NCOMP):
            piece = slice(part * NB, (part + 1) * NB)
            total = total + lax.dot_general(
                test_ref[0, :, piece],
                image[:, piece],
                (((0,), (0,)), ((), ())),
                preferred_element_type=jnp.float32,
            )
        out_ref[0, 0] = total


def pair_blocks(row_counts, col_counts, row_points, col_points, tests, bases):
    members, sources, width = tests.shape[0], bases.shape[0], tests.shape[2]
    grid_spec = pltpu.PrefetchScalarGridSpec(
        num_scalar_prefetch=2,
        grid=(members, sources, NMAX // row_tile),
        in_specs=[
            pl.BlockSpec((1, row_tile, 3), lambda m, s, t, *_: (m, t, 0)),
            pl.BlockSpec((1, 3, NMAX), lambda m, s, t, *_: (s, 0, 0)),
            pl.BlockSpec((1, row_tile, width), lambda m, s, t, *_: (m, t, 0)),
            pl.BlockSpec((1, NMAX, width), lambda m, s, t, *_: (s, 0, 0)),
        ],
        out_specs=pl.BlockSpec((1, 1, NB, NB), lambda m, s, t, *_: (m, s, 0, 0)),
        scratch_shapes=[pltpu.VMEM((row_tile, width), jnp.float32)],
    )
    return pl.pallas_call(
        pair_kernel,
        out_shape=jax.ShapeDtypeStruct((members, sources, NB, NB), jnp.float32),
        grid_spec=grid_spec,
        compiler_params=pltpu.CompilerParams(vmem_limit_bytes=32 * 1024 * 1024),
    )(row_counts, col_counts, row_points, col_points, tests, bases)


def from_owner(value, axis, owner):
    count = lax.axis_size(axis)
    place = (lax.axis_index(axis) - owner) % count
    reach = 1
    while reach < count:
        steps = [
            ((owner + n) % count, (owner + n + reach) % count)
            for n in range(min(reach, count - reach))
        ]
        arrived = lax.ppermute(value, axis, steps)
        value = jnp.where(place < reach, value, arrived)
        reach *= 2
    return value


def panel_kernel(block_ref, factor_ref, lower_ref, upper_ref):
    order = block_ref.shape[0]
    rows = lax.broadcasted_iota(jnp.int32, (order, order), 0)
    cols = lax.broadcasted_iota(jnp.int32, (order, order), 1)
    row_ids = lax.broadcasted_iota(jnp.int32, (order, 1), 0)
    lanes = lax.broadcasted_iota(jnp.int32, (1, order), 1)
    identity = jnp.where(rows == cols, 1.0, 0.0).astype(jnp.float32)
    factor_ref[...] = block_ref[...]
    lower_ref[...] = identity
    upper_ref[...] = identity

    def one_column(k, carry):
        current = factor_ref[...]
        row = factor_ref[pl.ds(k, 1), :]
        lower_row = lower_ref[pl.ds(k, 1), :]
        upper = upper_ref[...]
        at_column = cols == k
        pivot = jnp.sum(jnp.where(lanes == k, row, 0.0), axis=1, keepdims=True)
        column = jnp.sum(jnp.where(at_column, current, 0.0), axis=1, keepdims=True)
        upper_column = jnp.sum(jnp.where(at_column, upper, 0.0), axis=1, keepdims=True)
        multiplier = jnp.where(row_ids > k, column / pivot, 0.0)
        right = jnp.where(lanes > k, row, 0.0)
        factor_ref[...] = jnp.where(
            jnp.logical_and(at_column, rows > k), multiplier, current - multiplier * right
        )
        lower_ref[...] = lower_ref[...] - multiplier * lower_row
        upper_ref[...] = jnp.where(
            at_column, upper_column / pivot, upper - upper_column * (right / pivot)
        )
        return carry

    lax.fori_loop(0, order, one_column, 0)


def factor_panel(block):
    shape = jax.ShapeDtypeStruct(block.shape, jnp.float32)
    spec = pl.BlockSpec(memory_space=pltpu.VMEM)
    return pl.pallas_call(
        panel_kernel,
        out_shape=[shape] * 3,
        in_specs=[spec],
        out_specs=[spec] * 3,
        compiler_params=pltpu.CompilerParams(vmem_limit_bytes=16 * 1024 * 1024),
    )(block)


def local(basis, offsets, centers, patch_points, base):
    row_count = lax.axis_size("row")
    col_count = lax.axis_size("col")
    row_index = lax.axis_index("row")
    col_index = lax.axis_index("col")
    col_blocks = basis.shape[0]
    slice_len = basis.shape[2]
    width = basis.shape[3]
    row_blocks = NPATCH // row_count
    whole_cols, whole_offsets = (
        lax.all_gather(basis, "row", axis=2, tiled=True),
        lax.all_gather(offsets, "row", axis=3, tiled=True),
    )
    source_centers = lax.dynamic_index_in_dim(
        centers.reshape(col_blocks, col_count, 3), col_index, 1, keepdims=False
    )
    source_counts = lax.dynamic_index_in_dim(
        patch_points.reshape(col_blocks, col_count), col_index, 1, keepdims=False
    )
    source_points = source_centers[:, :, None] + whole_offsets[:, 0].astype(jnp.float32)
    source_live = jnp.arange(NMAX)[None, :] < source_counts[:, None]
    source_basis = jnp.where(source_live[:, :, None], whole_cols[:, 0], 0)
    sliced, sliced_offsets = (
        lax.all_gather(basis, "col", axis=1, tiled=True),
        lax.all_gather(offsets, "col", axis=1, tiled=True),
    )
    all_slices = sliced.reshape(NPATCH, slice_len, width)
    all_offsets = sliced_offsets.reshape(NPATCH, 3, slice_len)
    class_sizes = patch_points.reshape(row_blocks, row_count)
    class_order = jnp.argsort(-class_sizes, axis=0, stable=True)
    members = jnp.stack(
        [
            jnp.stack(
                [
                    class_order[member, (group - member) % row_count] * row_count
                    + (group - member) % row_count
                    for member in range(row_blocks)
                ]
            )
            for group in range(row_count)
        ]
    )
    flat_members = members.reshape(-1)
    turned_offsets = jnp.transpose(all_offsets, (0, 2, 1))

    def picked(array, ids):
        return jnp.stack(
            [lax.dynamic_index_in_dim(array, ids[n], 0, keepdims=False) for n in range(ids.shape[0])]
        )

    send_basis = picked(all_slices, flat_members)
    send_offsets = picked(turned_offsets, flat_members)
    got_basis, got_offsets = (
        lax.all_to_all(send_basis, "row", split_axis=0, concat_axis=1, tiled=True),
        lax.all_to_all(send_offsets, "row", split_axis=0, concat_axis=1, tiled=True),
    )
    mine = lax.dynamic_index_in_dim(members, row_index, 0, keepdims=False)
    my_counts = jnp.stack(
        [lax.dynamic_index_in_dim(patch_points, mine[n], 0, False) for n in range(row_blocks)]
    )
    member_points = picked(centers, mine)[:, None, :] + got_offsets.astype(jnp.float32)
    member_live = jnp.arange(NMAX)[None, :] < my_counts[:, None]
    tests = jnp.where(member_live[:, :, None], got_basis, 0)
    stacked = pair_blocks(
        my_counts, source_counts, member_points, source_points, tests, source_basis
    ).transpose(0, 2, 1, 3)
    slot_count = (row_blocks + row_count - 1) // row_count
    slot_ids = (np.arange(slot_count) * row_count)[None, :].astype(np.int32)
    peer_ids = jnp.arange(row_count, dtype=jnp.int32)[:, None]
    send_member = slot_ids + (row_index - peer_ids) % row_count
    send_valid = send_member < row_blocks
    outgoing = jnp.where(
        send_valid[:, :, None, None, None], picked(stacked, jnp.minimum(send_member, row_blocks - 1).reshape(-1)).reshape(
            send_member.shape + stacked.shape[1:]
        ), 0.0
    )
    incoming = lax.all_to_all(outgoing, "row", split_axis=0, concat_axis=0, tiled=True)
    recv_member = slot_ids + (peer_ids - row_index) % row_count
    recv_valid = recv_member < row_blocks
    my_order = lax.dynamic_index_in_dim(class_order, row_index, 1, keepdims=False)
    recv_block = jnp.sum(
        jnp.where(
            jnp.minimum(recv_member, row_blocks - 1)[:, :, None] == jnp.arange(row_blocks),
            my_order,
            0,
        ),
        axis=2,
    )
    landing = jnp.logical_and(
        recv_valid[None], recv_block[None] == jnp.arange(row_blocks)[:, None, None]
    ).astype(jnp.float32)
    reduced = jnp.einsum("agt,gtuqv->auqv", landing, incoming, precision=highest).reshape(
        row_blocks, 1, NB, col_blocks, NB
    )
    matrix = (base + reduced.reshape(row_blocks, 1, NB, col_blocks, 1, NB)).reshape(
        row_blocks * NB, col_blocks * NB
    )
    row_global = (
        (jnp.arange(row_blocks)[:, None] * row_count + row_index) * NB + jnp.arange(NB)[None, :]
    ).reshape(-1)
    col_global = (
        (jnp.arange(col_blocks)[:, None] * col_count + col_index) * NB + jnp.arange(NB)[None, :]
    ).reshape(-1)
    for panel_index in range(NPANEL):
        start = panel_index * PANEL
        finish = start + PANEL
        panel_span = start + jnp.arange(PANEL)
        pick_cols = (col_global[:, None] == panel_span[None, :]).astype(jnp.float32)
        pick_rows = (panel_span[:, None] == row_global[None, :]).astype(jnp.float32)
        col_part = jnp.dot(matrix, pick_cols, precision=highest)
        col_panel = from_owner(col_part, "col", panel_index % col_count)
        diagonal_part = jnp.dot(pick_rows, col_panel, precision=highest)
        row_part = jnp.dot(pick_rows, matrix, precision=highest)
        joined = jnp.concatenate([diagonal_part, row_part], axis=1)
        joined = from_owner(joined, "row", panel_index % row_count)
        diagonal_block, row_panel = joined[:, :PANEL], joined[:, PANEL:]
        factored_block, lower_inverse, upper_inverse = factor_panel(diagonal_block)
        left = jnp.dot(col_panel, upper_inverse, precision=highest)
        right = jnp.dot(lower_inverse, row_panel, precision=highest)
        left_kept = jnp.where((row_global >= finish)[:, None], left, 0.0)
        right_kept = jnp.where((col_global >= finish)[None, :], right, 0.0)
        matrix = matrix - jnp.dot(left_kept, right_kept, precision=highest)
        diagonal_rows = jnp.dot(pick_rows.T, factored_block, precision=highest)
        new_columns = jnp.where(
            (row_global < start)[:, None],
            col_panel,
            jnp.where((row_global < finish)[:, None], diagonal_rows, left),
        )
        in_columns = jnp.logical_and(col_global >= start, col_global < finish)
        matrix = jnp.where(
            in_columns[None, :], jnp.dot(new_columns, pick_cols.T, precision=highest), matrix
        )
        in_rows = jnp.logical_and(row_global >= start, row_global < finish)
        upper_rows = jnp.dot(pick_rows.T, right, precision=highest)
        matrix = jnp.where(
            jnp.logical_and(in_rows[:, None], (col_global >= finish)[None, :]), upper_rows, matrix
        )
    return matrix.reshape(row_blocks, 1, NB, col_blocks, 1, NB)


def solution(mesh):
    in_specs = (
        P(None, "col", "row", None),
        P(None, "col", None, "row"),
        P(),
        P(),
        P(None, "row", None, None, "col", None),
    )
    out_specs = P(None, "row", None, None, "col", None)
    return jax.shard_map(local, mesh=mesh, in_specs=in_specs, out_specs=out_specs, check_vma=False)
```

```python
import math

import jax
import jax.numpy as jnp
import numpy as np
from jax import lax
from jax.experimental import pallas as pl
from jax.experimental.pallas import tpu as pltpu
from jax.sharding import PartitionSpec as P

NB = 128
NCOMP = 3
NMAX = 1536
NPATCH = 16
PANEL = 128
NPANEL = 2


wave_number = 12.0
core_radius = 0.05
highest = lax.Precision.HIGHEST


cosine_series = (0.9999999890590201, -19.739204499453688, 64.93911745988827, -85.45013953077586, 60.16763095018129, -25.96759924584206, 6.528658157862129)
row_tile = 256
col_tile = 256


def pair_kernel(
    row_counts, col_counts, row_points_ref, col_points_ref, test_ref, basis_ref, out_ref, image_ref
):
    member, source, tile = pl.program_id(0), pl.program_id(1), pl.program_id(2)

    @pl.when(tile == 0)
    def _():
        out_ref[...] = jnp.zeros_like(out_ref)

    @pl.when(tile * row_tile < row_counts[member])
    def _():
        image_ref[...] = jnp.zeros_like(image_ref)
        row_points = row_points_ref[0]

        def one_chunk(chunk, carry):
            span = pl.ds(pl.multiple_of(chunk * col_tile, col_tile), col_tile)
            squared = jnp.zeros((row_tile, col_tile), jnp.float32)
            for axis in range(3):
                spacing = row_points[:, axis : axis + 1] - col_points_ref[0, axis : axis + 1, span]
                squared = squared + spacing * spacing
            distance = squared * lax.rsqrt(jnp.maximum(squared, 1e-30))
            turns = distance * (wave_number / (2.0 * math.pi))
            turns = turns - jnp.round(turns)
            square = turns * turns
            cosine = jnp.full_like(square, cosine_series[-1])
            for coefficient in cosine_series[-2::-1]:
                cosine = cosine * square + coefficient
            value = cosine * lax.rsqrt(squared + core_radius * core_radius)
            image_ref[...] += jnp.dot(
                value.astype(jnp.bfloat16), basis_ref[0, span, :], preferred_element_type=jnp.float32
            )
            return carry

        lax.fori_loop(0, (col_counts[source] + col_tile - 1) // col_tile, one_chunk, 0)
        image = image_ref[...].astype(jnp.bfloat16)
        total = out_ref[0, 0]
        for part in range(NCOMP):
            piece = slice(part * NB, (part + 1) * NB)
            total = total + lax.dot_general(
                test_ref[0, :, piece],
                image[:, piece],
                (((0,), (0,)), ((), ())),
                preferred_element_type=jnp.float32,
            )
        out_ref[0, 0] = total


def pair_blocks(row_counts, col_counts, row_points, col_points, tests, bases):
    members, sources, width = tests.shape[0], bases.shape[0], tests.shape[2]
    grid_spec = pltpu.PrefetchScalarGridSpec(
        num_scalar_prefetch=2,
        grid=(members, sources, NMAX // row_tile),
        in_specs=[
            pl.BlockSpec((1, row_tile, 3), lambda m, s, t, *_: (m, t, 0)),
            pl.BlockSpec((1, 3, NMAX), lambda m, s, t, *_: (s, 0, 0)),
            pl.BlockSpec((1, row_tile, width), lambda m, s, t, *_: (m, t, 0)),
            pl.BlockSpec((1, NMAX, width), lambda m, s, t, *_: (s, 0, 0)),
        ],
        out_specs=pl.BlockSpec((1, 1, NB, NB), lambda m, s, t, *_: (m, s, 0, 0)),
        scratch_shapes=[pltpu.VMEM((row_tile, width), jnp.float32)],
    )
    return pl.pallas_call(
        pair_kernel,
        out_shape=jax.ShapeDtypeStruct((members, sources, NB, NB), jnp.float32),
        grid_spec=grid_spec,
        compiler_params=pltpu.CompilerParams(vmem_limit_bytes=32 * 1024 * 1024),
    )(row_counts, col_counts, row_points, col_points, tests, bases)


def gather_direct(value, axis, dim):
    count, here, size = lax.axis_size(axis), lax.axis_index(axis), value.shape[dim]
    shape = list(value.shape)
    shape[dim] = size * count
    whole = lax.dynamic_update_slice_in_dim(
        jnp.zeros(shape, value.dtype), value, here * size, dim
    )
    arrivals = [
        lax.ppermute(value, axis, [(n, (n + shift) % count) for n in range(count)])
        for shift in range(1, count)
    ]
    for shift, arrived in enumerate(arrivals, 1):
        place = (here - shift) % count
        whole = lax.dynamic_update_slice_in_dim(whole, arrived, place * size, dim)
    return whole


def from_owner(value, axis, owner):
    count = lax.axis_size(axis)
    place = (lax.axis_index(axis) - owner) % count
    reach = 1
    while reach < count:
        steps = [
            ((owner + n) % count, (owner + n + reach) % count)
            for n in range(min(reach, count - reach))
        ]
        arrived = lax.ppermute(value, axis, steps)
        value = jnp.where(place < reach, value, arrived)
        reach *= 2
    return value


def panel_kernel(block_ref, factor_ref, lower_ref, upper_ref):
    order = block_ref.shape[0]
    rows = lax.broadcasted_iota(jnp.int32, (order, order), 0)
    cols = lax.broadcasted_iota(jnp.int32, (order, order), 1)
    row_ids = lax.broadcasted_iota(jnp.int32, (order, 1), 0)
    lanes = lax.broadcasted_iota(jnp.int32, (1, order), 1)
    identity = jnp.where(rows == cols, 1.0, 0.0).astype(jnp.float32)
    factor_ref[...] = block_ref[...]
    lower_ref[...] = identity
    upper_ref[...] = identity

    def one_column(k, carry):
        current = factor_ref[...]
        row = factor_ref[pl.ds(k, 1), :]
        lower_row = lower_ref[pl.ds(k, 1), :]
        upper = upper_ref[...]
        at_column = cols == k
        pivot = jnp.sum(jnp.where(lanes == k, row, 0.0), axis=1, keepdims=True)
        column = jnp.sum(jnp.where(at_column, current, 0.0), axis=1, keepdims=True)
        upper_column = jnp.sum(jnp.where(at_column, upper, 0.0), axis=1, keepdims=True)
        multiplier = jnp.where(row_ids > k, column / pivot, 0.0)
        right = jnp.where(lanes > k, row, 0.0)
        factor_ref[...] = jnp.where(
            jnp.logical_and(at_column, rows > k), multiplier, current - multiplier * right
        )
        lower_ref[...] = lower_ref[...] - multiplier * lower_row
        upper_ref[...] = jnp.where(
            at_column, upper_column / pivot, upper - upper_column * (right / pivot)
        )
        return carry

    lax.fori_loop(0, order, one_column, 0)


def factor_panel(block):
    shape = jax.ShapeDtypeStruct(block.shape, jnp.float32)
    spec = pl.BlockSpec(memory_space=pltpu.VMEM)
    return pl.pallas_call(
        panel_kernel,
        out_shape=[shape] * 3,
        in_specs=[spec],
        out_specs=[spec] * 3,
        compiler_params=pltpu.CompilerParams(vmem_limit_bytes=16 * 1024 * 1024),
    )(block)


def local(basis, offsets, centers, patch_points, base):
    row_count = lax.axis_size("row")
    col_count = lax.axis_size("col")
    row_index = lax.axis_index("row")
    col_index = lax.axis_index("col")
    col_blocks = basis.shape[0]
    slice_len = basis.shape[2]
    width = basis.shape[3]
    row_blocks = NPATCH // row_count
    whole_cols, whole_offsets = (
        gather_direct(basis, "row", 2),
        gather_direct(offsets, "row", 3),
    )
    source_centers = lax.dynamic_index_in_dim(
        centers.reshape(col_blocks, col_count, 3), col_index, 1, keepdims=False
    )
    source_counts = lax.dynamic_index_in_dim(
        patch_points.reshape(col_blocks, col_count), col_index, 1, keepdims=False
    )
    source_points = source_centers[:, :, None] + whole_offsets[:, 0].astype(jnp.float32)
    source_live = jnp.arange(NMAX)[None, :] < source_counts[:, None]
    source_basis = jnp.where(source_live[:, :, None], whole_cols[:, 0], 0)
    sliced, sliced_offsets = (
        lax.all_gather(basis, "col", axis=1, tiled=True),
        lax.all_gather(offsets, "col", axis=1, tiled=True),
    )
    all_slices = sliced.reshape(NPATCH, slice_len, width)
    all_offsets = sliced_offsets.reshape(NPATCH, 3, slice_len)
    class_sizes = patch_points.reshape(row_blocks, row_count)
    class_order = jnp.argsort(-class_sizes, axis=0, stable=True)
    members = jnp.stack(
        [
            jnp.stack(
                [
                    class_order[member, (group - member) % row_count] * row_count
                    + (group - member) % row_count
                    for member in range(row_blocks)
                ]
            )
            for group in range(row_count)
        ]
    )
    flat_members = members.reshape(-1)
    turned_offsets = jnp.transpose(all_offsets, (0, 2, 1))

    def picked(array, ids):
        return jnp.stack(
            [lax.dynamic_index_in_dim(array, ids[n], 0, keepdims=False) for n in range(ids.shape[0])]
        )

    send_basis = picked(all_slices, flat_members)
    send_offsets = picked(turned_offsets, flat_members)
    got_basis, got_offsets = (
        lax.all_to_all(send_basis, "row", split_axis=0, concat_axis=1, tiled=True),
        lax.all_to_all(send_offsets, "row", split_axis=0, concat_axis=1, tiled=True),
    )
    mine = lax.dynamic_index_in_dim(members, row_index, 0, keepdims=False)
    my_counts = jnp.stack(
        [lax.dynamic_index_in_dim(patch_points, mine[n], 0, False) for n in range(row_blocks)]
    )
    member_points = picked(centers, mine)[:, None, :] + got_offsets.astype(jnp.float32)
    member_live = jnp.arange(NMAX)[None, :] < my_counts[:, None]
    tests = jnp.where(member_live[:, :, None], got_basis, 0)
    stacked = pair_blocks(
        my_counts, source_counts, member_points, source_points, tests, source_basis
    ).transpose(0, 2, 1, 3)
    slot_count = (row_blocks + row_count - 1) // row_count
    slot_ids = (np.arange(slot_count) * row_count)[None, :].astype(np.int32)
    peer_ids = jnp.arange(row_count, dtype=jnp.int32)[:, None]
    send_member = slot_ids + (row_index - peer_ids) % row_count
    send_valid = send_member < row_blocks
    outgoing = jnp.where(
        send_valid[:, :, None, None, None], picked(stacked, jnp.minimum(send_member, row_blocks - 1).reshape(-1)).reshape(
            send_member.shape + stacked.shape[1:]
        ), 0.0
    )
    incoming = lax.all_to_all(outgoing, "row", split_axis=0, concat_axis=0, tiled=True)
    recv_member = slot_ids + (peer_ids - row_index) % row_count
    recv_valid = recv_member < row_blocks
    my_order = lax.dynamic_index_in_dim(class_order, row_index, 1, keepdims=False)
    recv_block = jnp.sum(
        jnp.where(
            jnp.minimum(recv_member, row_blocks - 1)[:, :, None] == jnp.arange(row_blocks),
            my_order,
            0,
        ),
        axis=2,
    )
    landing = jnp.logical_and(
        recv_valid[None], recv_block[None] == jnp.arange(row_blocks)[:, None, None]
    ).astype(jnp.float32)
    reduced = jnp.einsum("agt,gtuqv->auqv", landing, incoming, precision=highest).reshape(
        row_blocks, 1, NB, col_blocks, NB
    )
    matrix = (base + reduced.reshape(row_blocks, 1, NB, col_blocks, 1, NB)).reshape(
        row_blocks * NB, col_blocks * NB
    )
    row_global = (
        (jnp.arange(row_blocks)[:, None] * row_count + row_index) * NB + jnp.arange(NB)[None, :]
    ).reshape(-1)
    col_global = (
        (jnp.arange(col_blocks)[:, None] * col_count + col_index) * NB + jnp.arange(NB)[None, :]
    ).reshape(-1)
    for panel_index in range(NPANEL):
        start = panel_index * PANEL
        finish = start + PANEL
        panel_span = start + jnp.arange(PANEL)
        pick_cols = (col_global[:, None] == panel_span[None, :]).astype(jnp.float32)
        pick_rows = (panel_span[:, None] == row_global[None, :]).astype(jnp.float32)
        col_part = jnp.dot(matrix, pick_cols, precision=highest)
        col_panel = from_owner(col_part, "col", panel_index % col_count)
        diagonal_part = jnp.dot(pick_rows, col_panel, precision=highest)
        row_part = jnp.dot(pick_rows, matrix, precision=highest)
        joined = jnp.concatenate([diagonal_part, row_part], axis=1)
        joined = from_owner(joined, "row", panel_index % row_count)
        diagonal_block, row_panel = joined[:, :PANEL], joined[:, PANEL:]
        factored_block, lower_inverse, upper_inverse = factor_panel(diagonal_block)
        left = jnp.dot(col_panel, upper_inverse, precision=highest)
        right = jnp.dot(lower_inverse, row_panel, precision=highest)
        left_kept = jnp.where((row_global >= finish)[:, None], left, 0.0)
        right_kept = jnp.where((col_global >= finish)[None, :], right, 0.0)
        matrix = matrix - jnp.dot(left_kept, right_kept, precision=highest)
        diagonal_rows = jnp.dot(pick_rows.T, factored_block, precision=highest)
        new_columns = jnp.where(
            (row_global < start)[:, None],
            col_panel,
            jnp.where((row_global < finish)[:, None], diagonal_rows, left),
        )
        in_columns = jnp.logical_and(col_global >= start, col_global < finish)
        matrix = jnp.where(
            in_columns[None, :], jnp.dot(new_columns, pick_cols.T, precision=highest), matrix
        )
        in_rows = jnp.logical_and(row_global >= start, row_global < finish)
        upper_rows = jnp.dot(pick_rows.T, right, precision=highest)
        matrix = jnp.where(
            jnp.logical_and(in_rows[:, None], (col_global >= finish)[None, :]), upper_rows, matrix
        )
    return matrix.reshape(row_blocks, 1, NB, col_blocks, 1, NB)


def solution(mesh):
    in_specs = (
        P(None, "col", "row", None),
        P(None, "col", None, "row"),
        P(),
        P(),
        P(None, "row", None, None, "col", None),
    )
    out_specs = P(None, "row", None, None, "col", None)
    return jax.shard_map(local, mesh=mesh, in_specs=in_specs, out_specs=out_specs, check_vma=False)
```

```python
import math

import jax
import jax.numpy as jnp
import numpy as np
from jax import lax
from jax.experimental import pallas as pl
from jax.experimental.pallas import tpu as pltpu
from jax.sharding import PartitionSpec as P

NB = 128
NCOMP = 3
NMAX = 1536
NPATCH = 16
PANEL = 128
NPANEL = 2


wave_number = 12.0
core_radius = 0.05
highest = lax.Precision.HIGHEST


cosine_series = (0.9999999890590201, -19.739204499453688, 64.93911745988827, -85.45013953077586, 60.16763095018129, -25.96759924584206, 6.528658157862129)
row_tile = 256
col_tile = 256


def pair_kernel(
    row_counts, col_counts, row_points_ref, col_points_ref, test_ref, basis_ref, out_ref, image_ref
):
    member, source, tile = pl.program_id(0), pl.program_id(1), pl.program_id(2)

    @pl.when(tile == 0)
    def _():
        out_ref[...] = jnp.zeros_like(out_ref)

    @pl.when(tile * row_tile < row_counts[member])
    def _():
        image_ref[...] = jnp.zeros_like(image_ref)
        row_points = row_points_ref[0]

        def one_chunk(chunk, carry):
            span = pl.ds(pl.multiple_of(chunk * col_tile, col_tile), col_tile)
            squared = jnp.zeros((row_tile, col_tile), jnp.float32)
            for axis in range(3):
                spacing = row_points[:, axis : axis + 1] - col_points_ref[0, axis : axis + 1, span]
                squared = squared + spacing * spacing
            distance = squared * lax.rsqrt(jnp.maximum(squared, 1e-30))
            turns = distance * (wave_number / (2.0 * math.pi))
            turns = turns - jnp.round(turns)
            square = turns * turns
            cosine = jnp.full_like(square, cosine_series[-1])
            for coefficient in cosine_series[-2::-1]:
                cosine = cosine * square + coefficient
            value = cosine * lax.rsqrt(squared + core_radius * core_radius)
            image_ref[...] += jnp.dot(
                value.astype(jnp.bfloat16), basis_ref[0, span, :], preferred_element_type=jnp.float32
            )
            return carry

        lax.fori_loop(0, (col_counts[source] + col_tile - 1) // col_tile, one_chunk, 0)
        image = image_ref[...].astype(jnp.bfloat16)
        total = out_ref[0, 0]
        for part in range(NCOMP):
            piece = slice(part * NB, (part + 1) * NB)
            total = total + lax.dot_general(
                test_ref[0, :, piece],
                image[:, piece],
                (((0,), (0,)), ((), ())),
                preferred_element_type=jnp.float32,
            )
        out_ref[0, 0] = total


def pair_blocks(row_counts, col_counts, row_points, col_points, tests, bases):
    members, sources, width = tests.shape[0], bases.shape[0], tests.shape[2]
    grid_spec = pltpu.PrefetchScalarGridSpec(
        num_scalar_prefetch=2,
        grid=(members, sources, NMAX // row_tile),
        in_specs=[
            pl.BlockSpec((1, row_tile, 3), lambda m, s, t, *_: (m, t, 0)),
            pl.BlockSpec((1, 3, NMAX), lambda m, s, t, *_: (s, 0, 0)),
            pl.BlockSpec((1, row_tile, width), lambda m, s, t, *_: (m, t, 0)),
            pl.BlockSpec((1, NMAX, width), lambda m, s, t, *_: (s, 0, 0)),
        ],
        out_specs=pl.BlockSpec((1, 1, NB, NB), lambda m, s, t, *_: (m, s, 0, 0)),
        scratch_shapes=[pltpu.VMEM((row_tile, width), jnp.float32)],
    )
    return pl.pallas_call(
        pair_kernel,
        out_shape=jax.ShapeDtypeStruct((members, sources, NB, NB), jnp.float32),
        grid_spec=grid_spec,
        compiler_params=pltpu.CompilerParams(vmem_limit_bytes=32 * 1024 * 1024),
    )(row_counts, col_counts, row_points, col_points, tests, bases)


def gather_direct(value, axis, dim):
    count, here, size = lax.axis_size(axis), lax.axis_index(axis), value.shape[dim]
    shape = list(value.shape)
    shape[dim] = size * count
    whole = lax.dynamic_update_slice_in_dim(
        jnp.zeros(shape, value.dtype), value, here * size, dim
    )
    arrivals = [
        lax.ppermute(value, axis, [(n, (n + shift) % count) for n in range(count)])
        for shift in range(1, count)
    ]
    for shift, arrived in enumerate(arrivals, 1):
        place = (here - shift) % count
        whole = lax.dynamic_update_slice_in_dim(whole, arrived, place * size, dim)
    return whole


def from_owner(value, axis, owner):
    count = lax.axis_size(axis)
    place = (lax.axis_index(axis) - owner) % count
    reach = 1
    while reach < count:
        steps = [
            ((owner + n) % count, (owner + n + reach) % count)
            for n in range(min(reach, count - reach))
        ]
        arrived = lax.ppermute(value, axis, steps)
        value = jnp.where(place < reach, value, arrived)
        reach *= 2
    return value


def panel_kernel(block_ref, factor_ref, lower_ref, upper_ref):
    order = block_ref.shape[0]
    rows = lax.broadcasted_iota(jnp.int32, (order, order), 0)
    cols = lax.broadcasted_iota(jnp.int32, (order, order), 1)
    row_ids = lax.broadcasted_iota(jnp.int32, (order, 1), 0)
    lanes = lax.broadcasted_iota(jnp.int32, (1, order), 1)
    identity = jnp.where(rows == cols, 1.0, 0.0).astype(jnp.float32)
    factor_ref[...] = block_ref[...]
    lower_ref[...] = identity
    upper_ref[...] = identity

    def one_column(k, carry):
        current = factor_ref[...]
        row = factor_ref[pl.ds(k, 1), :]
        lower_row = lower_ref[pl.ds(k, 1), :]
        upper = upper_ref[...]
        at_column = cols == k
        pivot = jnp.sum(jnp.where(lanes == k, row, 0.0), axis=1, keepdims=True)
        column = jnp.sum(jnp.where(at_column, current, 0.0), axis=1, keepdims=True)
        upper_column = jnp.sum(jnp.where(at_column, upper, 0.0), axis=1, keepdims=True)
        multiplier = jnp.where(row_ids > k, column / pivot, 0.0)
        right = jnp.where(lanes > k, row, 0.0)
        factor_ref[...] = jnp.where(
            jnp.logical_and(at_column, rows > k), multiplier, current - multiplier * right
        )
        lower_ref[...] = lower_ref[...] - multiplier * lower_row
        upper_ref[...] = jnp.where(
            at_column, upper_column / pivot, upper - upper_column * (right / pivot)
        )
        return carry

    lax.fori_loop(0, order, one_column, 0)


def factor_panel(block):
    shape = jax.ShapeDtypeStruct(block.shape, jnp.float32)
    spec = pl.BlockSpec(memory_space=pltpu.VMEM)
    return pl.pallas_call(
        panel_kernel,
        out_shape=[shape] * 3,
        in_specs=[spec],
        out_specs=[spec] * 3,
        compiler_params=pltpu.CompilerParams(vmem_limit_bytes=16 * 1024 * 1024),
    )(block)


def local(basis, offsets, centers, patch_points, base):
    row_count = lax.axis_size("row")
    col_count = lax.axis_size("col")
    row_index = lax.axis_index("row")
    col_index = lax.axis_index("col")
    col_blocks = basis.shape[0]
    slice_len = basis.shape[2]
    width = basis.shape[3]
    row_blocks = NPATCH // row_count
    whole_cols, whole_offsets = (
        gather_direct(basis, "row", 2),
        gather_direct(offsets, "row", 3),
    )
    source_centers = lax.dynamic_index_in_dim(
        centers.reshape(col_blocks, col_count, 3), col_index, 1, keepdims=False
    )
    source_counts = lax.dynamic_index_in_dim(
        patch_points.reshape(col_blocks, col_count), col_index, 1, keepdims=False
    )
    source_points = source_centers[:, :, None] + whole_offsets[:, 0].astype(jnp.float32)
    source_live = jnp.arange(NMAX)[None, :] < source_counts[:, None]
    source_basis = jnp.where(source_live[:, :, None], whole_cols[:, 0], 0)
    sliced, sliced_offsets = (
        lax.all_gather(basis, "col", axis=1, tiled=True),
        lax.all_gather(offsets, "col", axis=1, tiled=True),
    )
    sliced, whole_cols = lax.optimization_barrier((sliced, whole_cols))
    all_slices = sliced.reshape(NPATCH, slice_len, width)
    all_offsets = sliced_offsets.reshape(NPATCH, 3, slice_len)
    class_sizes = patch_points.reshape(row_blocks, row_count)
    class_order = jnp.argsort(-class_sizes, axis=0, stable=True)
    members = jnp.stack(
        [
            jnp.stack(
                [
                    class_order[member, (group - member) % row_count] * row_count
                    + (group - member) % row_count
                    for member in range(row_blocks)
                ]
            )
            for group in range(row_count)
        ]
    )
    flat_members = members.reshape(-1)
    turned_offsets = jnp.transpose(all_offsets, (0, 2, 1))

    def picked(array, ids):
        return jnp.stack(
            [lax.dynamic_index_in_dim(array, ids[n], 0, keepdims=False) for n in range(ids.shape[0])]
        )

    send_basis = picked(all_slices, flat_members)
    send_offsets = picked(turned_offsets, flat_members)
    got_basis, got_offsets = (
        lax.all_to_all(send_basis, "row", split_axis=0, concat_axis=1, tiled=True),
        lax.all_to_all(send_offsets, "row", split_axis=0, concat_axis=1, tiled=True),
    )
    mine = lax.dynamic_index_in_dim(members, row_index, 0, keepdims=False)
    my_counts = jnp.stack(
        [lax.dynamic_index_in_dim(patch_points, mine[n], 0, False) for n in range(row_blocks)]
    )
    member_points = picked(centers, mine)[:, None, :] + got_offsets.astype(jnp.float32)
    member_live = jnp.arange(NMAX)[None, :] < my_counts[:, None]
    tests = jnp.where(member_live[:, :, None], got_basis, 0)
    stacked = pair_blocks(
        my_counts, source_counts, member_points, source_points, tests, source_basis
    ).transpose(0, 2, 1, 3)
    slot_count = (row_blocks + row_count - 1) // row_count
    slot_ids = (np.arange(slot_count) * row_count)[None, :].astype(np.int32)
    peer_ids = jnp.arange(row_count, dtype=jnp.int32)[:, None]
    send_member = slot_ids + (row_index - peer_ids) % row_count
    send_valid = send_member < row_blocks
    outgoing = jnp.where(
        send_valid[:, :, None, None, None], picked(stacked, jnp.minimum(send_member, row_blocks - 1).reshape(-1)).reshape(
            send_member.shape + stacked.shape[1:]
        ), 0.0
    )
    incoming = lax.all_to_all(outgoing, "row", split_axis=0, concat_axis=0, tiled=True)
    recv_member = slot_ids + (peer_ids - row_index) % row_count
    recv_valid = recv_member < row_blocks
    my_order = lax.dynamic_index_in_dim(class_order, row_index, 1, keepdims=False)
    recv_block = jnp.sum(
        jnp.where(
            jnp.minimum(recv_member, row_blocks - 1)[:, :, None] == jnp.arange(row_blocks),
            my_order,
            0,
        ),
        axis=2,
    )
    landing = jnp.logical_and(
        recv_valid[None], recv_block[None] == jnp.arange(row_blocks)[:, None, None]
    ).astype(jnp.float32)
    reduced = jnp.einsum("agt,gtuqv->auqv", landing, incoming, precision=highest).reshape(
        row_blocks, 1, NB, col_blocks, NB
    )
    matrix = (base + reduced.reshape(row_blocks, 1, NB, col_blocks, 1, NB)).reshape(
        row_blocks * NB, col_blocks * NB
    )
    row_global = (
        (jnp.arange(row_blocks)[:, None] * row_count + row_index) * NB + jnp.arange(NB)[None, :]
    ).reshape(-1)
    col_global = (
        (jnp.arange(col_blocks)[:, None] * col_count + col_index) * NB + jnp.arange(NB)[None, :]
    ).reshape(-1)
    for panel_index in range(NPANEL):
        start = panel_index * PANEL
        finish = start + PANEL
        panel_span = start + jnp.arange(PANEL)
        pick_cols = (col_global[:, None] == panel_span[None, :]).astype(jnp.float32)
        pick_rows = (panel_span[:, None] == row_global[None, :]).astype(jnp.float32)
        col_part = jnp.dot(matrix, pick_cols, precision=highest)
        col_panel = from_owner(col_part, "col", panel_index % col_count)
        diagonal_part = jnp.dot(pick_rows, col_panel, precision=highest)
        row_part = jnp.dot(pick_rows, matrix, precision=highest)
        joined = jnp.concatenate([diagonal_part, row_part], axis=1)
        joined = from_owner(joined, "row", panel_index % row_count)
        diagonal_block, row_panel = joined[:, :PANEL], joined[:, PANEL:]
        factored_block, lower_inverse, upper_inverse = factor_panel(diagonal_block)
        left = jnp.dot(col_panel, upper_inverse, precision=highest)
        right = jnp.dot(lower_inverse, row_panel, precision=highest)
        left_kept = jnp.where((row_global >= finish)[:, None], left, 0.0)
        right_kept = jnp.where((col_global >= finish)[None, :], right, 0.0)
        matrix = matrix - jnp.dot(left_kept, right_kept, precision=highest)
        diagonal_rows = jnp.dot(pick_rows.T, factored_block, precision=highest)
        new_columns = jnp.where(
            (row_global < start)[:, None],
            col_panel,
            jnp.where((row_global < finish)[:, None], diagonal_rows, left),
        )
        in_columns = jnp.logical_and(col_global >= start, col_global < finish)
        matrix = jnp.where(
            in_columns[None, :], jnp.dot(new_columns, pick_cols.T, precision=highest), matrix
        )
        in_rows = jnp.logical_and(row_global >= start, row_global < finish)
        upper_rows = jnp.dot(pick_rows.T, right, precision=highest)
        matrix = jnp.where(
            jnp.logical_and(in_rows[:, None], (col_global >= finish)[None, :]), upper_rows, matrix
        )
    return matrix.reshape(row_blocks, 1, NB, col_blocks, 1, NB)


def solution(mesh):
    in_specs = (
        P(None, "col", "row", None),
        P(None, "col", None, "row"),
        P(),
        P(),
        P(None, "row", None, None, "col", None),
    )
    out_specs = P(None, "row", None, None, "col", None)
    return jax.shard_map(local, mesh=mesh, in_specs=in_specs, out_specs=out_specs, check_vma=False)
```

```python
import math

import jax
import jax.numpy as jnp
import numpy as np
from jax import lax
from jax.experimental import pallas as pl
from jax.experimental.pallas import tpu as pltpu
from jax.sharding import PartitionSpec as P

NB = 128
NCOMP = 3
NMAX = 1536
NPATCH = 16
PANEL = 128
NPANEL = 2


wave_number = 12.0
core_radius = 0.05
highest = lax.Precision.HIGHEST


cosine_series = (0.9999999890590201, -19.739204499453688, 64.93911745988827, -85.45013953077586, 60.16763095018129, -25.96759924584206, 6.528658157862129)
row_tile = 256
col_tile = 256


def pair_kernel(
    row_counts, col_counts, row_points_ref, col_points_ref, test_ref, basis_ref, out_ref, image_ref
):
    member, source, tile = pl.program_id(0), pl.program_id(1), pl.program_id(2)

    @pl.when(tile == 0)
    def _():
        out_ref[...] = jnp.zeros_like(out_ref)

    @pl.when(tile * row_tile < row_counts[member])
    def _():
        image_ref[...] = jnp.zeros_like(image_ref)
        row_points = row_points_ref[0]

        def one_chunk(chunk, carry):
            span = pl.ds(pl.multiple_of(chunk * col_tile, col_tile), col_tile)
            squared = jnp.zeros((row_tile, col_tile), jnp.float32)
            for axis in range(3):
                spacing = row_points[:, axis : axis + 1] - col_points_ref[0, axis : axis + 1, span]
                squared = squared + spacing * spacing
            distance = squared * lax.rsqrt(jnp.maximum(squared, 1e-30))
            turns = distance * (wave_number / (2.0 * math.pi))
            turns = turns - jnp.round(turns)
            square = turns * turns
            cosine = jnp.full_like(square, cosine_series[-1])
            for coefficient in cosine_series[-2::-1]:
                cosine = cosine * square + coefficient
            value = cosine * lax.rsqrt(squared + core_radius * core_radius)
            image_ref[...] += jnp.dot(
                value.astype(jnp.bfloat16), basis_ref[0, span, :], preferred_element_type=jnp.float32
            )
            return carry

        lax.fori_loop(0, (col_counts[source] + col_tile - 1) // col_tile, one_chunk, 0)
        image = image_ref[...].astype(jnp.bfloat16)
        total = out_ref[0, 0]
        for part in range(NCOMP):
            piece = slice(part * NB, (part + 1) * NB)
            total = total + lax.dot_general(
                test_ref[0, :, piece],
                image[:, piece],
                (((0,), (0,)), ((), ())),
                preferred_element_type=jnp.float32,
            )
        out_ref[0, 0] = total


def pair_blocks(row_counts, col_counts, row_points, col_points, tests, bases):
    members, sources, width = tests.shape[0], bases.shape[0], tests.shape[2]
    grid_spec = pltpu.PrefetchScalarGridSpec(
        num_scalar_prefetch=2,
        grid=(members, sources, NMAX // row_tile),
        in_specs=[
            pl.BlockSpec((1, row_tile, 3), lambda m, s, t, *_: (m, t, 0)),
            pl.BlockSpec((1, 3, NMAX), lambda m, s, t, *_: (s, 0, 0)),
            pl.BlockSpec((1, row_tile, width), lambda m, s, t, *_: (m, t, 0)),
            pl.BlockSpec((1, NMAX, width), lambda m, s, t, *_: (s, 0, 0)),
        ],
        out_specs=pl.BlockSpec((1, 1, NB, NB), lambda m, s, t, *_: (m, s, 0, 0)),
        scratch_shapes=[pltpu.VMEM((row_tile, width), jnp.float32)],
    )
    return pl.pallas_call(
        pair_kernel,
        out_shape=jax.ShapeDtypeStruct((members, sources, NB, NB), jnp.float32),
        grid_spec=grid_spec,
        compiler_params=pltpu.CompilerParams(vmem_limit_bytes=32 * 1024 * 1024),
    )(row_counts, col_counts, row_points, col_points, tests, bases)


def gather_direct(value, axis, dim):
    count, here, size = lax.axis_size(axis), lax.axis_index(axis), value.shape[dim]
    shape = list(value.shape)
    shape[dim] = size * count
    whole = lax.dynamic_update_slice_in_dim(
        jnp.zeros(shape, value.dtype), value, here * size, dim
    )
    arrivals = [
        lax.ppermute(value, axis, [(n, (n + shift) % count) for n in range(count)])
        for shift in range(1, count)
    ]
    for shift, arrived in enumerate(arrivals, 1):
        place = (here - shift) % count
        whole = lax.dynamic_update_slice_in_dim(whole, arrived, place * size, dim)
    return whole


def from_owner(value, axis, owner):
    count = lax.axis_size(axis)
    place = (lax.axis_index(axis) - owner) % count
    reach = 1
    while reach < count:
        steps = [
            ((owner + n) % count, (owner + n + reach) % count)
            for n in range(min(reach, count - reach))
        ]
        arrived = lax.ppermute(value, axis, steps)
        value = jnp.where(place < reach, value, arrived)
        reach *= 2
    return value


def panel_kernel(block_ref, factor_ref, lower_ref, upper_ref):
    order = block_ref.shape[0]
    rows = lax.broadcasted_iota(jnp.int32, (order, order), 0)
    cols = lax.broadcasted_iota(jnp.int32, (order, order), 1)
    row_ids = lax.broadcasted_iota(jnp.int32, (order, 1), 0)
    lanes = lax.broadcasted_iota(jnp.int32, (1, order), 1)
    identity = jnp.where(rows == cols, 1.0, 0.0).astype(jnp.float32)
    factor_ref[...] = block_ref[...]
    lower_ref[...] = identity
    upper_ref[...] = identity

    def one_column(k, carry):
        current = factor_ref[...]
        row = factor_ref[pl.ds(k, 1), :]
        lower_row = lower_ref[pl.ds(k, 1), :]
        upper = upper_ref[...]
        at_column = cols == k
        pivot = jnp.sum(jnp.where(lanes == k, row, 0.0), axis=1, keepdims=True)
        column = jnp.sum(jnp.where(at_column, current, 0.0), axis=1, keepdims=True)
        upper_column = jnp.sum(jnp.where(at_column, upper, 0.0), axis=1, keepdims=True)
        multiplier = jnp.where(row_ids > k, column / pivot, 0.0)
        right = jnp.where(lanes > k, row, 0.0)
        factor_ref[...] = jnp.where(
            jnp.logical_and(at_column, rows > k), multiplier, current - multiplier * right
        )
        lower_ref[...] = lower_ref[...] - multiplier * lower_row
        upper_ref[...] = jnp.where(
            at_column, upper_column / pivot, upper - upper_column * (right / pivot)
        )
        return carry

    lax.fori_loop(0, order, one_column, 0)


def factor_panel(block):
    shape = jax.ShapeDtypeStruct(block.shape, jnp.float32)
    spec = pl.BlockSpec(memory_space=pltpu.VMEM)
    return pl.pallas_call(
        panel_kernel,
        out_shape=[shape] * 3,
        in_specs=[spec],
        out_specs=[spec] * 3,
        compiler_params=pltpu.CompilerParams(vmem_limit_bytes=16 * 1024 * 1024),
    )(block)


def local(basis, offsets, centers, patch_points, base):
    row_count = lax.axis_size("row")
    col_count = lax.axis_size("col")
    row_index = lax.axis_index("row")
    col_index = lax.axis_index("col")
    col_blocks = basis.shape[0]
    slice_len = basis.shape[2]
    width = basis.shape[3]
    row_blocks = NPATCH // row_count
    whole_cols, whole_offsets = (
        gather_direct(basis, "row", 2),
        gather_direct(offsets, "row", 3),
    )
    source_centers = lax.dynamic_index_in_dim(
        centers.reshape(col_blocks, col_count, 3), col_index, 1, keepdims=False
    )
    source_counts = lax.dynamic_index_in_dim(
        patch_points.reshape(col_blocks, col_count), col_index, 1, keepdims=False
    )
    source_points = source_centers[:, :, None] + whole_offsets[:, 0].astype(jnp.float32)
    source_live = jnp.arange(NMAX)[None, :] < source_counts[:, None]
    sliced, sliced_offsets = (
        lax.all_gather(basis, "col", axis=1, tiled=True),
        lax.all_gather(offsets, "col", axis=1, tiled=True),
    )
    sliced, whole_cols = lax.optimization_barrier((sliced, whole_cols))
    source_basis = jnp.where(source_live[:, :, None], whole_cols[:, 0], 0)
    all_slices = sliced.reshape(NPATCH, slice_len, width)
    all_offsets = sliced_offsets.reshape(NPATCH, 3, slice_len)
    class_sizes = patch_points.reshape(row_blocks, row_count)
    class_order = jnp.argsort(-class_sizes, axis=0, stable=True)
    members = jnp.stack(
        [
            jnp.stack(
                [
                    class_order[member, (group - member) % row_count] * row_count
                    + (group - member) % row_count
                    for member in range(row_blocks)
                ]
            )
            for group in range(row_count)
        ]
    )
    flat_members = members.reshape(-1)
    turned_offsets = jnp.transpose(all_offsets, (0, 2, 1))

    def picked(array, ids):
        return jnp.stack(
            [lax.dynamic_index_in_dim(array, ids[n], 0, keepdims=False) for n in range(ids.shape[0])]
        )

    send_basis = picked(all_slices, flat_members)
    send_offsets = picked(turned_offsets, flat_members)
    got_basis, got_offsets = (
        lax.all_to_all(send_basis, "row", split_axis=0, concat_axis=1, tiled=True),
        lax.all_to_all(send_offsets, "row", split_axis=0, concat_axis=1, tiled=True),
    )
    mine = lax.dynamic_index_in_dim(members, row_index, 0, keepdims=False)
    my_counts = jnp.stack(
        [lax.dynamic_index_in_dim(patch_points, mine[n], 0, False) for n in range(row_blocks)]
    )
    member_points = picked(centers, mine)[:, None, :] + got_offsets.astype(jnp.float32)
    member_live = jnp.arange(NMAX)[None, :] < my_counts[:, None]
    tests = jnp.where(member_live[:, :, None], got_basis, 0)
    stacked = pair_blocks(
        my_counts, source_counts, member_points, source_points, tests, source_basis
    ).transpose(0, 2, 1, 3)
    slot_count = (row_blocks + row_count - 1) // row_count
    slot_ids = (np.arange(slot_count) * row_count)[None, :].astype(np.int32)
    peer_ids = jnp.arange(row_count, dtype=jnp.int32)[:, None]
    send_member = slot_ids + (row_index - peer_ids) % row_count
    send_valid = send_member < row_blocks
    outgoing = jnp.where(
        send_valid[:, :, None, None, None], picked(stacked, jnp.minimum(send_member, row_blocks - 1).reshape(-1)).reshape(
            send_member.shape + stacked.shape[1:]
        ), 0.0
    )
    incoming = lax.all_to_all(outgoing, "row", split_axis=0, concat_axis=0, tiled=True)
    recv_member = slot_ids + (peer_ids - row_index) % row_count
    recv_valid = recv_member < row_blocks
    my_order = lax.dynamic_index_in_dim(class_order, row_index, 1, keepdims=False)
    recv_block = jnp.sum(
        jnp.where(
            jnp.minimum(recv_member, row_blocks - 1)[:, :, None] == jnp.arange(row_blocks),
            my_order,
            0,
        ),
        axis=2,
    )
    landing = jnp.logical_and(
        recv_valid[None], recv_block[None] == jnp.arange(row_blocks)[:, None, None]
    ).astype(jnp.float32)
    reduced = jnp.einsum("agt,gtuqv->auqv", landing, incoming, precision=highest).reshape(
        row_blocks, 1, NB, col_blocks, NB
    )
    matrix = (base + reduced.reshape(row_blocks, 1, NB, col_blocks, 1, NB)).reshape(
        row_blocks * NB, col_blocks * NB
    )
    row_global = (
        (jnp.arange(row_blocks)[:, None] * row_count + row_index) * NB + jnp.arange(NB)[None, :]
    ).reshape(-1)
    col_global = (
        (jnp.arange(col_blocks)[:, None] * col_count + col_index) * NB + jnp.arange(NB)[None, :]
    ).reshape(-1)
    for panel_index in range(NPANEL):
        start = panel_index * PANEL
        finish = start + PANEL
        panel_span = start + jnp.arange(PANEL)
        pick_cols = (col_global[:, None] == panel_span[None, :]).astype(jnp.float32)
        pick_rows = (panel_span[:, None] == row_global[None, :]).astype(jnp.float32)
        col_part = jnp.dot(matrix, pick_cols, precision=highest)
        col_panel = from_owner(col_part, "col", panel_index % col_count)
        diagonal_part = jnp.dot(pick_rows, col_panel, precision=highest)
        row_part = jnp.dot(pick_rows, matrix, precision=highest)
        joined = jnp.concatenate([diagonal_part, row_part], axis=1)
        joined = from_owner(joined, "row", panel_index % row_count)
        diagonal_block, row_panel = joined[:, :PANEL], joined[:, PANEL:]
        factored_block, lower_inverse, upper_inverse = factor_panel(diagonal_block)
        left = jnp.dot(col_panel, upper_inverse, precision=highest)
        right = jnp.dot(lower_inverse, row_panel, precision=highest)
        left_kept = jnp.where((row_global >= finish)[:, None], left, 0.0)
        right_kept = jnp.where((col_global >= finish)[None, :], right, 0.0)
        matrix = matrix - jnp.dot(left_kept, right_kept, precision=highest)
        diagonal_rows = jnp.dot(pick_rows.T, factored_block, precision=highest)
        new_columns = jnp.where(
            (row_global < start)[:, None],
            col_panel,
            jnp.where((row_global < finish)[:, None], diagonal_rows, left),
        )
        in_columns = jnp.logical_and(col_global >= start, col_global < finish)
        matrix = jnp.where(
            in_columns[None, :], jnp.dot(new_columns, pick_cols.T, precision=highest), matrix
        )
        in_rows = jnp.logical_and(row_global >= start, row_global < finish)
        upper_rows = jnp.dot(pick_rows.T, right, precision=highest)
        matrix = jnp.where(
            jnp.logical_and(in_rows[:, None], (col_global >= finish)[None, :]), upper_rows, matrix
        )
    return matrix.reshape(row_blocks, 1, NB, col_blocks, 1, NB)


def solution(mesh):
    in_specs = (
        P(None, "col", "row", None),
        P(None, "col", None, "row"),
        P(),
        P(),
        P(None, "row", None, None, "col", None),
    )
    out_specs = P(None, "row", None, None, "col", None)
    return jax.shard_map(local, mesh=mesh, in_specs=in_specs, out_specs=out_specs, check_vma=False)
```
